512 devices in a mesh: dp: 32 (over z, x_lo, core), ctx: 16 (over x_hi, y).
Axes of the slice: x: 4 (x_hi: 2, x_lo: 2; x = x_hi * 2 + x_lo), y: 8, z: 8, core: 2. Of those that a mesh axis runs over, the one named last changes fastest.
Arguments:
- activations: bfloat16 [65536, 8192], P(('dp', 'ctx')), may hold values from -24 to 24
- gradients: bfloat16 [65536, 8192], P(('dp', 'ctx')), may hold values from -24 to 24
- valid_rows: int32 [32], replicated, may hold values from 1024 to 2048, as said below
Outputs:
- factor_a: float32 [384, 2, 4096], P('dp', None, 'ctx')
- factor_g: float32 [384, 2, 4096], P('dp', None, 'ctx')
The draws below stay inside these ranges and needn't reach their ends.
Inputs may be any that keep to these rules, and one draw needn't show every extreme that they name: Each group's live rows are the first valid_rows[q] rows of its 2048 rows; some group has all rows live and some group exactly half.
All inputs are finite; a program needn't handle non-finite values.
Results may differ from the reference program's by a relative error of at most 0.0012.
Values may be sent and summed in bfloat16 or wider, within the bound.
A program may use at most 128 MiB of HBM per device.

```python
import jax
import jax.numpy as jnp
from jax import lax

D = 8192
WIN = 384
ROW_DEV = 128
ROWS = 65536
N_DP = 32
N_CTX = 16


def draw_valid_rows(key, part):
    key = jax.random.fold_in(key, 7)
    window = ROW_DEV * N_CTX
    values = jax.random.randint(key, (N_DP,), window // 2, window + 1)
    values = values.at[0].set(window).at[1].set(window // 2)
    return values.astype(jnp.int32)


def spiked(result, key, source, target, blocks, factor):
    def block_of(dim):
        return (jnp.arange(result.shape[dim]) // (result.shape[dim] // blocks)).reshape((-1,) + (1,) * (result.ndim - 1 - dim))

    one_side = jax.random.permutation(key, blocks)[block_of(target)]
    far = (block_of(target) + blocks // 2) % blocks
    return jnp.where((block_of(source) == one_side) | (block_of(source) == far), factor * result, result)


def steps_of(own_key, dims, shards, low, high):
    def one(axis_at, shards_of):
        draws = jax.random.uniform(jax.random.fold_in(jax.random.fold_in(own_key, 6), axis_at), (shards_of,), jnp.float32, low / len(shards), high / len(shards))
        return jnp.repeat(jnp.exp(draws), dims[axis_at] // shards_of).reshape((-1,) + (1,) * (len(dims) - axis_at - 1))

    loudness = one(*shards[0])
    for cut in shards[1:]:
        loudness = loudness * one(*cut)
    return loudness


def bell_draw_with(stream_key, shape, deviation, limit, pieces, heavy, kind=jnp.bfloat16):
    drawn = deviation * jax.random.normal(stream_key, shape, jnp.float32)
    if pieces:
        drawn = drawn * steps_of(stream_key, shape, pieces, -0.22, 0.18)
    return jnp.clip(spiked(drawn, jax.random.fold_in(stream_key, 3), *heavy), -limit, limit).astype(kind)


def setup_inputs(seed: int = 0) -> dict:
    key_list = jax.random.split(jax.random.key(seed), 4)
    activations = bell_draw_with(key_list[0], (ROWS, D), 1.0, 24.0, ((0, 512),), (0, 1, 512, 6.0))
    gradients = bell_draw_with(key_list[1], (ROWS, D), 1.0, 24.0, ((0, 512),), (0, 1, 512, 6.0))
    valid_rows = draw_valid_rows(jax.random.fold_in(key_list[3], 71), 0)
    return {"activations": activations, "gradients": gradients, "valid_rows": valid_rows}


def block_products(rows_a, rows_g, live_rows):
    positions = jnp.arange(ROW_DEV, dtype=jnp.int32)
    keep = (positions < live_rows).astype(rows_a.dtype)[:, None]
    masked_a = rows_a * keep
    masked_g = rows_g * keep
    contract = (((0,), (0,)), ((), ()))
    part_a = lax.dot_general(masked_a[:, :WIN], masked_a, contract, preferred_element_type=jnp.float32)
    part_g = lax.dot_general(masked_g[:, :WIN], masked_g, contract, preferred_element_type=jnp.float32)
    return part_a.astype(jnp.bfloat16).astype(jnp.float32), part_g.astype(jnp.bfloat16).astype(jnp.float32)


def reference(activations, gradients, valid_rows):
    blocks_a = activations.reshape(N_DP, N_CTX, ROW_DEV, D)
    blocks_g = gradients.reshape(N_DP, N_CTX, ROW_DEV, D)
    row_total = jnp.sum(valid_rows).astype(jnp.float32)
    empty = jnp.zeros((WIN, D), jnp.float32)

    def one_group(carry, item):
        group_a, group_g, group_valid = item

        def one_block(acc, block):
            rows_a, rows_g, ctx_index = block
            live_rows = jnp.clip(group_valid - ctx_index * ROW_DEV, 0, ROW_DEV).astype(jnp.int32)
            part_a, part_g = block_products(rows_a, rows_g, live_rows)
            return (acc[0] + part_a, acc[1] + part_g), None

        indices = jnp.arange(N_CTX, dtype=jnp.int32)
        (sum_a, sum_g), _ = lax.scan(one_block, (empty, empty), (group_a, group_g, indices))
        return (carry[0] + sum_a, carry[1] + sum_g), None

    (factor_a, factor_g), _ = lax.scan(one_group, (empty, empty), (blocks_a, blocks_g, valid_rows))
    factor_a = (factor_a / row_total).reshape(WIN, 2, D // 2)
    factor_g = (factor_g / row_total).reshape(WIN, 2, D // 2)
    return factor_a, factor_g
```

```python
import jax
import jax.numpy as jnp
from jax import lax
from jax.experimental import pallas as pl
from jax.experimental.pallas import tpu as pltpu
from jax.sharding import PartitionSpec as P

MESH = pl.DeviceIdType.MESH
F32, BF16 = jnp.float32, jnp.bfloat16
WIN, ROWS, TILE = 384, 128, 256
NX, NY, NZ = 4, 8, 8
HALF = 16
AXES = {"x": (0, NX), "y": (1, NY), "z": (2, NZ)}
PARTS = ("y", "z", "x")
ROW0 = {"y": 0, "z": 128, "x": 256}
SECOND = {("y", 0): "x", ("y", 1): "x", ("z", 0): "x", ("z", 1): "x", ("x", 0): "y", ("x", 1): "z"}
LAST = {"z": (("y", 0), ("y", 1), ("x", 0)), "y": (("z", 0), ("z", 1), ("x", 1))}
STREAMS = tuple(SECOND)


def place():
    dp, ctx = lax.axis_index("dp"), lax.axis_index("ctx")
    x = lax.div(ctx, 8) * 2 + lax.rem(lax.div(dp, 2), 2)
    return x, lax.rem(ctx, 8), lax.div(dp, 4), lax.rem(dp, 2)


def device(x, y, z, core):
    return (z * 4 + lax.rem(x, 2) * 2 + core, lax.div(x, 2) * 8 + y)


def chain_length(n, half, way):
    return n // 2 if half == way else n // 2 - 1


def kernel(
    rows_ref, acts, grads, out_a, out_g,
    held, wins, prods, send_y, recv_y, send_z, recv_z, send_x, recv_x,
    sums, send_two, recv_two, three, recv_three, last_send, last_recv,
    own_sem, in_send, in_recv, y_send, y_recv, z_send, z_recv, x_send, x_recv,
    two_send, two_recv, three_send, three_recv, last_sem,
):
    here = place()
    x, y, z, core = here
    partner = device(x, y, z, 1 - core)

    def moved(axis, by):
        at, n = AXES[axis]
        there = list(here)
        there[at] = lax.rem(here[at] + (by % n), n)
        return there[at], device(*there)

    def own_copy(array, h):
        cols = pl.ds(h * 4096, 4096)
        return pltpu.make_async_copy(array.at[:, cols], held.at[0, :, cols], own_sem.at[h])

    def swap_copy(array, h):
        cols = pl.ds(h * 4096, 4096)
        return pltpu.make_async_remote_copy(
            src_ref=array.at[:, cols], dst_ref=held.at[1, :, cols], send_sem=in_send.at[h], recv_sem=in_recv.at[h],
            device_id=partner, device_id_type=MESH,
        )

    @pl.when(core == 0)
    def _():
        for h in range(2):
            own_copy(acts, h).start()

    @pl.when(core == 1)
    def _():
        for h in range(2):
            own_copy(grads, h).start()

    barrier = pltpu.get_barrier_semaphore()
    peers = [partner] + [moved(axis, by)[1] for axis in "xyz" for by in range(1, AXES[axis][1])]
    for peer in peers:
        pl.semaphore_signal(barrier, inc=1, device_id=peer, device_id_type=MESH)
    pl.semaphore_wait(barrier, len(peers))

    @pl.when(core == 0)
    def _():
        for h in range(2):
            swap_copy(grads, h).start()

    @pl.when(core == 1)
    def _():
        for h in range(2):
            swap_copy(acts, h).start()

    ctx = lax.axis_index("ctx")
    group = lax.axis_index("dp")

    def window(k, group):
        live = rows_ref[group] - ctx * ROWS
        keep = lax.broadcasted_iota(jnp.int32, (ROWS, WIN), 0) < live
        win = jnp.where(keep, held[k, :, :WIN].astype(F32), 0.0).T
        for i, part in enumerate(PARTS):
            order = [(zz, lo) for zz in range(8) for lo in range(2)]
            if part != "z":
                order = [(zz, lo) for lo in range(2) for zz in range(8)]
            at = [zz * 48 + lo * 24 + i * 8 for zz, lo in order]
            wins[k, ROW0[part] : ROW0[part] + 128, :] = jnp.concatenate([win[r : r + 8] for r in at]).astype(BF16)

    def products(h):
        def one(i, carry):
            t = h * HALF + i
            total = None
            for k in range(2):
                cols = held[k, :, pl.ds(pl.multiple_of(t * TILE, TILE), TILE)]
                part = jnp.dot(wins[k], cols, preferred_element_type=F32).astype(BF16).astype(F32)
                total = part if total is None else total + part
            prods[t] = total
            return carry

        lax.fori_loop(0, HALF, one, 0)

    def own(part, h, dest):
        base = h * HALF
        if part == "y":
            return jnp.stack([prods[base + hi * 8 + dest, 0:128, :] for hi in range(2)])
        if part == "z":
            return prods[pl.ds(base, HALF), pl.ds(pl.multiple_of(128 + dest * 16, 16), 16), :]
        at = pl.multiple_of(256 + lax.rem(dest, 2) * 64, 64)
        return prods[pl.ds(base + lax.div(dest, 2) * 8, 8), pl.ds(at, 64), :]

    chain = {"y": (send_y, recv_y, y_send, y_recv), "z": (send_z, recv_z, z_send, z_recv), "x": (send_x, recv_x, x_send, x_recv)}

    def chain_copy(part, h, way, k):
        src, dst, ssem, rsem = chain[part]
        return pltpu.make_async_remote_copy(
            src_ref=src.at[h, way, k - 1], dst_ref=dst.at[h, way, k - 1], send_sem=ssem.at[h, way, k - 1],
            recv_sem=rsem.at[h, way, k - 1], device_id=moved(part, 1 if way == 0 else -1)[1], device_id_type=MESH,
        )

    def hop(part, h, way, k):
        n = AXES[part][1]
        dest, _ = moved(part, k if way == 0 else -k)
        value = own(part, h, dest)
        if k < chain_length(n, h, way):
            chain_copy(part, h, way, k + 1).wait_recv()
            value = value + chain[part][1][h, way, k].astype(F32)
        chain[part][0][h, way, k - 1] = value.astype(BF16)
        chain_copy(part, h, way, k).start()

    def finish(part, h):
        for way in range(2):
            chain_copy(part, h, way, 1).wait_recv()
        value = own(part, h, here[AXES[part][0]])
        for way in range(2):
            value = value + chain[part][1][h, way, 0].astype(F32)
        s = STREAMS.index((part, h))
        if part == "y":
            sums[s, 0:4] = value.reshape(4, 64, TILE)
        elif part == "z":
            for hi in range(2):
                for yy in range(8):
                    sums[s, hi * 2 : hi * 2 + 2, yy * 8 : yy * 8 + 8, :] = value[hi * 8 + yy].reshape(2, 8, TILE)
        elif h == 0:
            sums[s] = value
        else:
            for yy in range(8):
                sums[s, :, yy * 8 : yy * 8 + 8, :] = value[yy].reshape(8, 8, TILE)

    def far_first(n):
        return sorted(range(1, n), key=lambda k: -min(k, n - k))

    def two_copy(s, k):
        return pltpu.make_async_remote_copy(
            src_ref=send_two.at[s, k - 1], dst_ref=recv_two.at[s, k - 1], send_sem=two_send.at[s, k - 1],
            recv_sem=two_recv.at[s, k - 1], device_id=moved(SECOND[STREAMS[s]], k)[1], device_id_type=MESH,
        )

    def spread(s):
        axis = SECOND[STREAMS[s]]
        for k in far_first(AXES[axis][1]):
            send_two[s, k - 1] = sums[s, moved(axis, k)[0]].astype(BF16)
            two_copy(s, k).start()

    def gather(s):
        at, n = AXES[SECOND[STREAMS[s]]]
        value = sums[s, here[at]]
        for k in range(1, n):
            two_copy(s, k).wait_recv()
            value = value + recv_two[s, k - 1].astype(F32)
        for g, axis in enumerate(("z", "y")):
            if STREAMS[s] in LAST[axis]:
                three[g, :, LAST[axis].index(STREAMS[s])] = value.reshape(8, 8, TILE)

    def three_copy(g, k):
        dest, there = moved("zy"[g], k)
        return pltpu.make_async_remote_copy(
            src_ref=three.at[g, dest], dst_ref=recv_three.at[g, k - 1], send_sem=three_send.at[g, k - 1],
            recv_sem=three_recv.at[g, k - 1], device_id=there, device_id_type=MESH,
        )

    own_copy(acts, 0).wait()
    window(0, group)
    swap_copy(acts, 0).wait_recv()
    window(1, group + 1 - 2 * core)
    products(0)
    for part in "zyx":
        hop(part, 0, 0, AXES[part][1] // 2)
    own_copy(acts, 1).wait()
    swap_copy(acts, 1).wait_recv()
    products(1)
    for part in "zyx":
        hop(part, 1, 1, AXES[part][1] // 2)
    for part in "zyx":
        n = AXES[part][1]
        hop(part, 1, 0, n // 2 - 1)
        hop(part, 0, 1, n // 2 - 1)
    for slot in range(2, 7):
        for part in "zy":
            k = 4 - slot // 2
            if slot % 2 == 0:
                hop(part, 0, 0, k)
                hop(part, 1, 1, k)
            else:
                hop(part, 1, 0, k - 1)
                hop(part, 0, 1, k - 1)
        if slot == 3:
            hop("x", 0, 0, 1)
            hop("x", 1, 1, 1)

    for part in "xyz":
        for h in range(2):
            finish(part, h)
            spread(STREAMS.index((part, h)))
    for s in (4, 5, 0, 1, 2, 3):
        gather(s)
    for k in far_first(8):
        for g in range(2):
            three_copy(g, k).start()

    total = rows_ref[0]
    for i in range(1, 32):
        total = total + rows_ref[i]
    total = total.astype(F32)
    done = []
    for g in range(2):
        value = three[g, here[AXES["zy"[g]][0]]]
        for k in range(1, 8):
            three_copy(g, k).wait_recv()
            value = value + recv_three[g, k - 1]
        done.append(value)
    kept = []
    for h in range(2):
        block = jnp.concatenate([done[0][h], done[1][h], done[h][2]]) / total
        low, high = block[0:12], block[12:24]
        pad = jnp.zeros((4, TILE), F32)
        last_send[h] = jnp.concatenate([jnp.where(core == 0, high, low), pad])
        kept.append(jnp.where(core == 0, low, high))
    last = pltpu.make_async_remote_copy(
        src_ref=last_send, dst_ref=last_recv, send_sem=last_sem.at[0], recv_sem=last_sem.at[1], device_id=partner, device_id_type=MESH
    )
    last.start()

    for h in range(2):
        swap_copy(acts, h).wait_send()
    for part in PARTS:
        for h in range(2):
            for way in range(2):
                for k in range(1, chain_length(AXES[part][1], h, way) + 1):
                    chain_copy(part, h, way, k).wait_send()
    for s, stream in enumerate(STREAMS):
        for k in range(1, AXES[SECOND[stream]][1]):
            two_copy(s, k).wait_send()
    for g in range(2):
        for k in range(1, 8):
            three_copy(g, k).wait_send()
    last.wait()
    for h in range(2):
        came = last_recv[h, 0:12]
        out_a[h] = jnp.where(core == 0, kept[h], came)
        out_g[h] = jnp.where(core == 0, came, kept[h])


def body(activations, gradients, valid_rows):
    dma = pltpu.SemaphoreType.DMA
    out = jax.ShapeDtypeStruct((2, 12, TILE), F32)
    y_shape, z_shape, x_shape = (2, 2, 4, 2, 128, TILE), (2, 2, 4, HALF, 16, TILE), (2, 2, 2, 8, 64, TILE)
    a, g = pl.pallas_call(
        kernel,
        out_shape=(out, out),
        in_specs=[
            pl.BlockSpec(memory_space=pltpu.SMEM),
            pl.BlockSpec(memory_space=pl.ANY),
            pl.BlockSpec(memory_space=pl.ANY),
        ],
        out_specs=(pl.BlockSpec(memory_space=pltpu.VMEM),) * 2,
        scratch_shapes=[
            pltpu.VMEM((2, ROWS, 8192), BF16),
            pltpu.VMEM((2, WIN, ROWS), BF16),
            pltpu.VMEM((2 * HALF, WIN, TILE), F32),
            pltpu.VMEM(y_shape, BF16), pltpu.VMEM(y_shape, BF16),
            pltpu.VMEM(z_shape, BF16), pltpu.VMEM(z_shape, BF16),
            pltpu.VMEM(x_shape, BF16), pltpu.VMEM(x_shape, BF16),
            pltpu.VMEM((6, 8, 64, TILE), F32),
            pltpu.VMEM((6, 7, 64, TILE), BF16), pltpu.VMEM((6, 7, 64, TILE), BF16),
            pltpu.VMEM((2, 8, 3, 8, TILE), F32), pltpu.VMEM((2, 7, 3, 8, TILE), F32),
            pltpu.VMEM((2, 16, TILE), F32), pltpu.VMEM((2, 16, TILE), F32),
            dma((2,)), dma((2,)), dma((2,)),
            dma((2, 2, 4)), dma((2, 2, 4)), dma((2, 2, 4)), dma((2, 2, 4)), dma((2, 2, 2)), dma((2, 2, 2)),
            dma((6, 7)), dma((6, 7)), dma((2, 7)), dma((2, 7)), dma((2,)),
        ],
        compiler_params=pltpu.CompilerParams(collective_id=0, has_side_effects=True, vmem_limit_bytes=56 * 2**20),
        cost_estimate=pl.CostEstimate(flops=2 * 384 * 256 * 8192, bytes_accessed=4 * 2**20, transcendentals=0),
    )(valid_rows, activations, gradients)
    return jnp.transpose(a, (1, 0, 2)), jnp.transpose(g, (1, 0, 2))


def solution(mesh):
    placed = (P(("dp", "ctx"), None), P(("dp", "ctx"), None), P())
    return jax.shard_map(
        body,
        mesh=mesh,
        in_specs=placed,
        out_specs=(P("dp", None, "ctx"), P("dp", None, "ctx")),
        check_vma=False,
    )
```

```python
import jax
import jax.numpy as jnp
from jax import lax
from jax.experimental import pallas as pl
from jax.experimental.pallas import tpu as pltpu
from jax.sharding import PartitionSpec as P

MESH = pl.DeviceIdType.MESH
F32, BF16 = jnp.float32, jnp.bfloat16
WIN, ROWS, TILE = 384, 128, 256
NX, NY, NZ = 4, 8, 8
AXES = {"x": (0, NX), "y": (1, NY), "z": (2, NZ)}
PARTS = ("y", "z", "x")
ROW0 = {"y": 0, "z": 128, "x": 256}
SECOND = {("y", 0): "x", ("y", 1): "x", ("z", 0): "x", ("z", 1): "x", ("x", 0): "y", ("x", 1): "z"}
LAST = {"z": (("y", 0), ("y", 1), ("x", 0)), "y": (("z", 0), ("z", 1), ("x", 1))}
STREAMS = tuple(SECOND)


def place():
    dp, ctx = lax.axis_index("dp"), lax.axis_index("ctx")
    x = lax.div(ctx, 8) * 2 + lax.rem(lax.div(dp, 2), 2)
    return x, lax.rem(ctx, 8), lax.div(dp, 4), lax.rem(dp, 2)


def device(x, y, z, core):
    return (z * 4 + lax.rem(x, 2) * 2 + core, lax.div(x, 2) * 8 + y)


def chain_length(n, q, way):
    return n // 2 if q % 2 == way else n // 2 - 1


def kernel(
    rows_ref, acts, grads, out,
    held, wins, prods, send_y, recv_y, send_z, recv_z, send_x, recv_x,
    sums, send_two, recv_two, three, recv_three, last_send, last_recv,
    own_sem, in_send, in_recv, y_send, y_recv, z_send, z_recv, x_send, x_recv,
    two_send, two_recv, three_send, three_recv, last_sem,
):
    here = place()
    x, y, z, core = here
    partner = device(x, y, z, 1 - core)

    def moved(axis, by):
        at, n = AXES[axis]
        there = list(here)
        there[at] = lax.rem(here[at] + (by % n), n)
        return there[at], device(*there)

    def own_copy(array, q):
        cols = pl.ds(q * 2048, 2048)
        return pltpu.make_async_copy(array.at[:, cols], held.at[0, :, cols], own_sem.at[q])

    def swap_copy(array, q):
        cols = pl.ds(q * 2048, 2048)
        return pltpu.make_async_remote_copy(
            src_ref=array.at[:, cols], dst_ref=held.at[1, :, cols], send_sem=in_send.at[q], recv_sem=in_recv.at[q],
            device_id=partner, device_id_type=MESH,
        )

    @pl.when(core == 0)
    def _():
        for q in range(4):
            own_copy(acts, q).start()

    @pl.when(core == 1)
    def _():
        for q in range(4):
            own_copy(grads, q).start()

    barrier = pltpu.get_barrier_semaphore()
    peers = [partner] + [moved(axis, by)[1] for axis in "xyz" for by in range(1, AXES[axis][1])]
    for peer in peers:
        pl.semaphore_signal(barrier, inc=1, device_id=peer, device_id_type=MESH)

    def swap():
        pl.semaphore_wait(barrier, len(peers))

        @pl.when(core == 0)
        def _():
            for q in range(4):
                swap_copy(grads, q).start()

        @pl.when(core == 1)
        def _():
            for q in range(4):
                swap_copy(acts, q).start()

    ctx = lax.axis_index("ctx")
    group = lax.axis_index("dp")

    def window(k, group):
        live = rows_ref[group] - ctx * ROWS
        keep = lax.broadcasted_iota(jnp.int32, (ROWS, WIN), 0) < live
        win = jnp.where(keep, held[k, :, :WIN].astype(F32), 0.0).T
        for i, part in enumerate(PARTS):
            order = [(zz, lo) for zz in range(8) for lo in range(2)]
            if part != "z":
                order = [(zz, lo) for lo in range(2) for zz in range(8)]
            at = [zz * 48 + lo * 24 + i * 8 for zz, lo in order]
            wins[k, ROW0[part] : ROW0[part] + 128, :] = jnp.concatenate([win[r : r + 8] for r in at]).astype(BF16)

    def products(k, q):
        def one(i, carry):
            t = q * 8 + i
            cols = held[k, :, pl.ds(pl.multiple_of(t * TILE, TILE), TILE)]
            prods[k, t] = jnp.dot(wins[k], cols, preferred_element_type=F32).astype(BF16)
            return carry

        lax.fori_loop(0, 8, one, 0, unroll=2)

    def own(part, q, dest):
        def half(k):
            if part == "y":
                return prods[k, q * 8 + dest, 0:128, :].astype(F32)
            if part == "z":
                return prods[k, q * 8 : q * 8 + 8, pl.ds(pl.multiple_of(128 + dest * 16, 16), 16), :].astype(F32)
            at = pl.multiple_of(256 + lax.rem(dest, 2) * 64, 64)
            tile = (q // 2) * 16 + lax.div(dest, 2) * 8 + (q % 2) * 4
            return prods[k, pl.ds(tile, 4), pl.ds(at, 64), :].astype(F32)

        return half(0) + half(1)

    chain = {"y": (send_y, recv_y, y_send, y_recv), "z": (send_z, recv_z, z_send, z_recv), "x": (send_x, recv_x, x_send, x_recv)}

    def chain_copy(part, q, way, k):
        src, dst, ssem, rsem = chain[part]
        return pltpu.make_async_remote_copy(
            src_ref=src.at[q, way, k - 1], dst_ref=dst.at[q, way, k - 1], send_sem=ssem.at[q, way, k - 1],
            recv_sem=rsem.at[q, way, k - 1], device_id=moved(part, 1 if way == 0 else -1)[1], device_id_type=MESH,
        )

    def hop(part, q, way, k):
        n = AXES[part][1]
        dest, _ = moved(part, k if way == 0 else -k)
        value = own(part, q, dest)
        if k < chain_length(n, q, way):
            chain_copy(part, q, way, k + 1).wait_recv()
            value = value + chain[part][1][q, way, k].astype(F32)
        chain[part][0][q, way, k - 1] = value.astype(BF16)
        chain_copy(part, q, way, k).start()

    def finish(part, q):
        for way in range(2):
            chain_copy(part, q, way, 1).wait_recv()
        value = own(part, q, here[AXES[part][0]])
        for way in range(2):
            value = value + chain[part][1][q, way, 0].astype(F32)
        h, low = q // 2, q % 2
        s = STREAMS.index((part, h))
        if part == "y":
            sums[s, low * 2 : low * 2 + 2] = value.reshape(2, 64, TILE)
        elif part == "z":
            for yy in range(8):
                sums[s, low * 2 : low * 2 + 2, yy * 8 : yy * 8 + 8, :] = value[yy].reshape(2, 8, TILE)
        elif h == 0:
            sums[s, low * 4 : low * 4 + 4] = value
        else:
            for i in range(4):
                at = (low * 4 + i) * 8
                sums[s, :, at : at + 8, :] = value[i].reshape(8, 8, TILE)

    def far_first(n):
        return sorted(range(1, n), key=lambda k: -min(k, n - k))

    def two_copy(s, k):
        return pltpu.make_async_remote_copy(
            src_ref=send_two.at[s, k - 1], dst_ref=recv_two.at[s, k - 1], send_sem=two_send.at[s, k - 1],
            recv_sem=two_recv.at[s, k - 1], device_id=moved(SECOND[STREAMS[s]], k)[1], device_id_type=MESH,
        )

    def spread(s):
        axis = SECOND[STREAMS[s]]
        for k in far_first(AXES[axis][1]):
            send_two[s, k - 1] = sums[s, moved(axis, k)[0]].astype(BF16)
            two_copy(s, k).start()

    def gather(s):
        at, n = AXES[SECOND[STREAMS[s]]]
        value = sums[s, here[at]]
        for k in range(1, n):
            two_copy(s, k).wait_recv()
            value = value + recv_two[s, k - 1].astype(F32)
        for g, axis in enumerate(("z", "y")):
            if STREAMS[s] in LAST[axis]:
                three[g, :, LAST[axis].index(STREAMS[s])] = value.reshape(8, 8, TILE)

    def three_copy(g, k):
        dest, there = moved("zy"[g], k)
        return pltpu.make_async_remote_copy(
            src_ref=three.at[g, dest], dst_ref=recv_three.at[g, k - 1], send_sem=three_send.at[g, k - 1],
            recv_sem=three_recv.at[g, k - 1], device_id=there, device_id_type=MESH,
        )

    for q in range(4):
        own_copy(acts, q).wait()
        if q == 0:
            window(0, group)
        products(0, q)
        if q == 1:
            swap()
    for q in range(4):
        swap_copy(acts, q).wait_recv()
        if q == 0:
            window(1, group + 1 - 2 * core)
        products(1, q)
        far = q % 2
        for part in "zy":
            hop(part, q, far, 4)
            hop(part, q, 1 - far, 3)
        if q % 2 == 1:
            for low in range(2):
                hop("x", q - 1 + low, low, 2)
                hop("x", q - 1 + low, 1 - low, 1)
    for k in (3, 2, 1):
        for q in range(4):
            for part in "zy":
                hop(part, q, q % 2, k)
            if k == 2:
                hop("x", q, q % 2, 1)
        if k > 1:
            for q in range(4):
                for part in "zy":
                    hop(part, q, 1 - q % 2, k - 1)

    for part in "xyz":
        for h in range(2):
            for q in (2 * h, 2 * h + 1):
                finish(part, q)
            spread(STREAMS.index((part, h)))
    for q in range(4):
        swap_copy(acts, q).wait_send()
    for part in PARTS:
        for q in range(4):
            for way in range(2):
                for k in range(1, chain_length(AXES[part][1], q, way) + 1):
                    chain_copy(part, q, way, k).wait_send()
    for s in (0, 1, 2, 3, 4, 5):
        gather(s)
    for k in far_first(8):
        for g in range(2):
            three_copy(g, k).start()
    for s, stream in enumerate(STREAMS):
        for k in range(1, AXES[SECOND[stream]][1]):
            two_copy(s, k).wait_send()

    total = rows_ref[0]
    for i in range(1, 32):
        total = total + rows_ref[i]
    total = total.astype(F32)
    done = []
    for g in range(2):
        value = three[g, here[AXES["zy"[g]][0]]]
        for k in range(1, 8):
            three_copy(g, k).wait_recv()
            value = value + recv_three[g, k - 1]
        done.append(value)
    kept = []
    for h in range(2):
        block = jnp.concatenate([done[0][h], done[1][h], done[h][2]]) / total
        low, high = block[0:12], block[12:24]
        pad = jnp.zeros((4, TILE), F32)
        last_send[h] = jnp.concatenate([jnp.where(core == 0, high, low), pad])
        kept.append(jnp.where(core == 0, low, high))
    last = pltpu.make_async_remote_copy(
        src_ref=last_send, dst_ref=last_recv, send_sem=last_sem.at[0], recv_sem=last_sem.at[1], device_id=partner, device_id_type=MESH
    )
    last.start()

    for g in range(2):
        for k in range(1, 8):
            three_copy(g, k).wait_send()
    last.wait()
    for h in range(2):
        came = last_recv[h, 0:12]
        out[0, h] = jnp.where(core == 0, kept[h], came)
        out[1, h] = jnp.where(core == 0, came, kept[h])


def arrange(both, out_a, out_g):
    for h in range(2):
        out_a[:, h, :] = both[0, h]
        out_g[:, h, :] = both[1, h]


def body(activations, gradients, valid_rows):
    dma = pltpu.SemaphoreType.DMA
    vmem = pl.BlockSpec(memory_space=pltpu.VMEM)
    y_shape, z_shape, x_shape = (4, 2, 4, 128, TILE), (4, 2, 4, 8, 16, TILE), (4, 2, 2, 4, 64, TILE)
    both = pl.pallas_call(
        kernel,
        out_shape=jax.ShapeDtypeStruct((2, 2, 12, TILE), F32),
        in_specs=[
            pl.BlockSpec(memory_space=pltpu.SMEM),
            pl.BlockSpec(memory_space=pl.ANY),
            pl.BlockSpec(memory_space=pl.ANY),
        ],
        out_specs=vmem,
        scratch_shapes=[
            pltpu.VMEM((2, ROWS, 8192), BF16),
            pltpu.VMEM((2, WIN, ROWS), BF16),
            pltpu.VMEM((2, 32, WIN, TILE), BF16),
            pltpu.VMEM(y_shape, BF16), pltpu.VMEM(y_shape, BF16),
            pltpu.VMEM(z_shape, BF16), pltpu.VMEM(z_shape, BF16),
            pltpu.VMEM(x_shape, BF16), pltpu.VMEM(x_shape, BF16),
            pltpu.VMEM((6, 8, 64, TILE), F32),
            pltpu.VMEM((6, 7, 64, TILE), BF16), pltpu.VMEM((6, 7, 64, TILE), BF16),
            pltpu.VMEM((2, 8, 3, 8, TILE), F32), pltpu.VMEM((2, 7, 3, 8, TILE), F32),
            pltpu.VMEM((2, 16, TILE), F32), pltpu.VMEM((2, 16, TILE), F32),
            dma((4,)), dma((4,)), dma((4,)),
            dma((4, 2, 4)), dma((4, 2, 4)), dma((4, 2, 4)), dma((4, 2, 4)), dma((4, 2, 2)), dma((4, 2, 2)),
            dma((6, 7)), dma((6, 7)), dma((2, 7)), dma((2, 7)), dma((2,)),
        ],
        compiler_params=pltpu.CompilerParams(collective_id=0, has_side_effects=True, vmem_limit_bytes=56 * 2**20),
        cost_estimate=pl.CostEstimate(flops=2 * 384 * 256 * 8192, bytes_accessed=4 * 2**20, transcendentals=0),
    )(valid_rows, activations, gradients)
    out = jax.ShapeDtypeStruct((12, 2, TILE), F32)
    return pl.pallas_call(arrange, out_shape=(out, out), in_specs=[vmem], out_specs=(vmem, vmem))(both)


def solution(mesh):
    placed = (P(("dp", "ctx"), None), P(("dp", "ctx"), None), P())
    return jax.shard_map(
        body,
        mesh=mesh,
        in_specs=placed,
        out_specs=(P("dp", None, "ctx"), P("dp", None, "ctx")),
        check_vma=False,
    )
```

```python
import jax
import jax.numpy as jnp
from jax import lax
from jax.experimental import pallas as pl
from jax.experimental.pallas import tpu as pltpu
from jax.sharding import PartitionSpec as P

MESH = pl.DeviceIdType.MESH
F32, BF16 = jnp.float32, jnp.bfloat16
WIN, ROWS, TILE = 384, 128, 256
NX, NY, NZ = 4, 8, 8
AXES = {"x": (0, NX), "y": (1, NY), "z": (2, NZ)}
PARTS = ("y", "z", "x")
ROW0 = {"y": 0, "z": 128, "x": 256}
SECOND = {("y", 0): "x", ("y", 1): "x", ("z", 0): "x", ("z", 1): "x", ("x", 0): "y", ("x", 1): "z"}
LAST = {"z": (("y", 0), ("y", 1), ("x", 0)), "y": (("z", 0), ("z", 1), ("x", 1))}
STREAMS = tuple(SECOND)


def place():
    dp, ctx = lax.axis_index("dp"), lax.axis_index("ctx")
    x = lax.div(ctx, 8) * 2 + lax.rem(lax.div(dp, 2), 2)
    return x, lax.rem(ctx, 8), lax.div(dp, 4), lax.rem(dp, 2)


def device(x, y, z, core):
    return (z * 4 + lax.rem(x, 2) * 2 + core, lax.div(x, 2) * 8 + y)


def chain_length(n, q, way):
    return n // 2 if q % 2 == way else n // 2 - 1


def kernel(
    live, acts, grads, out,
    rows_ref, held, wins, prods, send_y, recv_y, send_z, recv_z, send_x, recv_x,
    sums, send_two, recv_two, three, recv_three, last_send, last_recv,
    live_sem, own_sem, in_send, in_recv, y_send, y_recv, z_send, z_recv, x_send, x_recv,
    two_send, two_recv, three_send, three_recv, last_sem,
):
    here = place()
    x, y, z, core = here
    partner = device(x, y, z, 1 - core)

    def moved(axis, by):
        at, n = AXES[axis]
        there = list(here)
        there[at] = lax.rem(here[at] + (by % n), n)
        return there[at], device(*there)

    def own_copy(array, q):
        cols = pl.ds(q * 2048, 2048)
        return pltpu.make_async_copy(array.at[:, cols], held.at[0, :, cols], own_sem.at[q])

    def swap_copy(array, q):
        cols = pl.ds(q * 2048, 2048)
        return pltpu.make_async_remote_copy(
            src_ref=array.at[:, cols], dst_ref=held.at[1, :, cols], send_sem=in_send, recv_sem=in_recv.at[q],
            device_id=partner, device_id_type=MESH,
        )

    @pl.when(core == 0)
    def _():
        for q in range(4):
            own_copy(acts, q).start()

    @pl.when(core == 1)
    def _():
        for q in range(4):
            own_copy(grads, q).start()

    live_copy = pltpu.make_async_copy(live, rows_ref, live_sem)
    live_copy.start()
    barrier = pltpu.get_barrier_semaphore()
    peers = [partner] + [moved(axis, by)[1] for axis in "xyz" for by in range(1, AXES[axis][1])]
    for peer in peers:
        pl.semaphore_signal(barrier, inc=1, device_id=peer, device_id_type=MESH)

    def swap():
        pl.semaphore_wait(barrier, len(peers))

        @pl.when(core == 0)
        def _():
            for q in range(4):
                swap_copy(grads, q).start()

        @pl.when(core == 1)
        def _():
            for q in range(4):
                swap_copy(acts, q).start()

    ctx = lax.axis_index("ctx")
    group = lax.axis_index("dp")

    def window(k, group):
        live = rows_ref[group] - ctx * ROWS
        keep = lax.broadcasted_iota(jnp.int32, (ROWS, WIN), 0) < live
        win = jnp.where(keep, held[k, :, :WIN].astype(F32), 0.0).T
        for i, part in enumerate(PARTS):
            order = [(zz, lo) for zz in range(8) for lo in range(2)]
            if part != "z":
                order = [(zz, lo) for lo in range(2) for zz in range(8)]
            at = [zz * 48 + lo * 24 + i * 8 for zz, lo in order]
            wins[k, ROW0[part] : ROW0[part] + 128, :] = jnp.concatenate([win[r : r + 8] for r in at]).astype(BF16)

    def products(k, q):
        def one(i, carry):
            t = q * 8 + i
            cols = held[k, :, pl.ds(pl.multiple_of(t * TILE, TILE), TILE)]
            prods[k, t] = jnp.dot(wins[k], cols, preferred_element_type=F32).astype(BF16)
            return carry

        lax.fori_loop(0, 8, one, 0, unroll=2)

    def own(part, q, dest):
        def half(k):
            if part == "y":
                return prods[k, q * 8 + dest, 0:128, :].astype(F32)
            if part == "z":
                return prods[k, q * 8 : q * 8 + 8, pl.ds(pl.multiple_of(128 + dest * 16, 16), 16), :].astype(F32)
            at = pl.multiple_of(256 + lax.rem(dest, 2) * 64, 64)
            tile = (q // 2) * 16 + lax.div(dest, 2) * 8 + (q % 2) * 4
            return prods[k, pl.ds(tile, 4), pl.ds(at, 64), :].astype(F32)

        return half(0) + half(1)

    chain = {"y": (send_y, recv_y, y_send, y_recv), "z": (send_z, recv_z, z_send, z_recv), "x": (send_x, recv_x, x_send, x_recv)}

    def drain(ref, sem):
        pltpu.make_async_copy(ref, ref, sem).wait()

    def slot(part, q, way, k):
        far = AXES[part][1] // 2
        return q * (2 * far - 1) + (0 if q % 2 == way else far) + k - 1

    def chain_copy(part, q, way, k):
        src, dst, ssem, rsem = chain[part]
        at = slot(part, q, way, k)
        return pltpu.make_async_remote_copy(
            src_ref=src.at[at], dst_ref=dst.at[at], send_sem=ssem, recv_sem=rsem.at[at],
            device_id=moved(part, 1 if way == 0 else -1)[1], device_id_type=MESH,
        )

    def hop(part, q, way, k):
        n = AXES[part][1]
        dest, _ = moved(part, k if way == 0 else -k)
        value = own(part, q, dest)
        if k < chain_length(n, q, way):
            chain_copy(part, q, way, k + 1).wait_recv()
            value = value + chain[part][1][slot(part, q, way, k + 1)].astype(F32)
        chain[part][0][slot(part, q, way, k)] = value.astype(BF16)
        chain_copy(part, q, way, k).start()

    def finish(part, q):
        for way in range(2):
            chain_copy(part, q, way, 1).wait_recv()
        value = own(part, q, here[AXES[part][0]])
        for way in range(2):
            value = value + chain[part][1][slot(part, q, way, 1)].astype(F32)
        h, low = q // 2, q % 2
        s = STREAMS.index((part, h))
        if part == "y":
            sums[s, low * 2 : low * 2 + 2] = value.reshape(2, 64, TILE)
        elif part == "z":
            for yy in range(8):
                sums[s, low * 2 : low * 2 + 2, yy * 8 : yy * 8 + 8, :] = value[yy].reshape(2, 8, TILE)
        elif h == 0:
            sums[s, low * 4 : low * 4 + 4] = value
        else:
            for i in range(4):
                at = (low * 4 + i) * 8
                sums[s, :, at : at + 8, :] = value[i].reshape(8, 8, TILE)

    def far_first(n):
        return sorted(range(1, n), key=lambda k: -min(k, n - k))

    def two_copy(s, k):
        return pltpu.make_async_remote_copy(
            src_ref=send_two.at[s, k - 1], dst_ref=recv_two.at[s, k - 1], send_sem=two_send.at[s],
            recv_sem=two_recv.at[s], device_id=moved(SECOND[STREAMS[s]], k)[1], device_id_type=MESH,
        )

    def spread(s):
        axis = SECOND[STREAMS[s]]
        for k in far_first(AXES[axis][1]):
            send_two[s, k - 1] = sums[s, moved(axis, k)[0]].astype(BF16)
            two_copy(s, k).start()

    def gather(s):
        at, n = AXES[SECOND[STREAMS[s]]]
        value = sums[s, here[at]]
        drain(recv_two.at[s, pl.ds(0, n - 1)], two_recv.at[s])
        for k in range(1, n):
            value = value + recv_two[s, k - 1].astype(F32)
        for g, axis in enumerate(("z", "y")):
            if STREAMS[s] in LAST[axis]:
                three[g, :, LAST[axis].index(STREAMS[s])] = value.reshape(8, 8, TILE)

    def three_copy(g, k):
        dest, there = moved("zy"[g], k)
        return pltpu.make_async_remote_copy(
            src_ref=three.at[g, dest], dst_ref=recv_three.at[g, k - 1], send_sem=three_send.at[g],
            recv_sem=three_recv.at[g], device_id=there, device_id_type=MESH,
        )

    swap()
    live_copy.wait()
    for q in range(4):
        own_copy(acts, q).wait()
        if q == 0:
            window(0, group)
            products(0, 0)
        if q == 1:
            products(0, 1)
    for q in range(4):
        if q > 1:
            products(0, q)
        swap_copy(acts, q).wait_recv()
        if q == 0:
            window(1, group + 1 - 2 * core)
        products(1, q)
        far = q % 2
        for part in "zy":
            hop(part, q, far, 4)
            hop(part, q, 1 - far, 3)
        if q % 2 == 1:
            for low in range(2):
                hop("x", q - 1 + low, low, 2)
                hop("x", q - 1 + low, 1 - low, 1)
    for k in (3, 2, 1):
        for q in range(4):
            for part in "zy":
                hop(part, q, q % 2, k)
            if k == 2:
                hop("x", q, q % 2, 1)
        if k > 1:
            for q in range(4):
                for part in "zy":
                    hop(part, q, 1 - q % 2, k - 1)

    for part in "xyz":
        for h in range(2):
            for q in (2 * h, 2 * h + 1):
                finish(part, q)
            spread(STREAMS.index((part, h)))
    drain(held.at[1], in_send)
    for part in PARTS:
        drain(chain[part][0], chain[part][2])
    for s in (0, 1, 2, 3, 4, 5):
        gather(s)
    for k in far_first(8):
        for g in range(2):
            three_copy(g, k).start()
    for s, stream in enumerate(STREAMS):
        drain(send_two.at[s, pl.ds(0, AXES[SECOND[stream]][1] - 1)], two_send.at[s])

    total = rows_ref[0]
    for i in range(1, 32):
        total = total + rows_ref[i]
    total = total.astype(F32)
    done = []
    for g in range(2):
        value = three[g, here[AXES["zy"[g]][0]]]
        drain(recv_three.at[g], three_recv.at[g])
        for k in range(1, 8):
            value = value + recv_three[g, k - 1]
        done.append(value)
    kept = []
    for h in range(2):
        block = jnp.concatenate([done[0][h], done[1][h], done[h][2]]) / total
        low, high = block[0:12], block[12:24]
        pad = jnp.zeros((4, TILE), F32)
        last_send[h] = jnp.concatenate([jnp.where(core == 0, high, low), pad])
        kept.append(jnp.where(core == 0, low, high))
    last = pltpu.make_async_remote_copy(
        src_ref=last_send, dst_ref=last_recv, send_sem=last_sem.at[0], recv_sem=last_sem.at[1], device_id=partner, device_id_type=MESH
    )
    last.start()

    for g in range(2):
        drain(recv_three.at[g], three_send.at[g])
    last.wait()
    for h in range(2):
        came = last_recv[h, 0:12]
        out[0, h] = jnp.where(core == 0, kept[h], came)
        out[1, h] = jnp.where(core == 0, came, kept[h])


def arrange(both, out_a, out_g):
    for h in range(2):
        out_a[:, h, :] = both[0, h]
        out_g[:, h, :] = both[1, h]


def body(activations, gradients, valid_rows):
    dma = pltpu.SemaphoreType.DMA
    vmem = pl.BlockSpec(memory_space=pltpu.VMEM)
    y_shape, z_shape, x_shape = (28, 128, TILE), (28, 8, 16, TILE), (12, 4, 64, TILE)
    both = pl.pallas_call(
        kernel,
        out_shape=jax.ShapeDtypeStruct((2, 2, 12, TILE), F32),
        in_specs=[
            pl.BlockSpec(memory_space=pl.ANY),
            pl.BlockSpec(memory_space=pl.ANY),
            pl.BlockSpec(memory_space=pl.ANY),
        ],
        out_specs=vmem,
        scratch_shapes=[
            pltpu.SMEM((32,), jnp.int32),
            pltpu.VMEM((2, ROWS, 8192), BF16),
            pltpu.VMEM((2, WIN, ROWS), BF16),
            pltpu.VMEM((2, 32, WIN, TILE), BF16),
            pltpu.VMEM(y_shape, BF16), pltpu.VMEM(y_shape, BF16),
            pltpu.VMEM(z_shape, BF16), pltpu.VMEM(z_shape, BF16),
            pltpu.VMEM(x_shape, BF16), pltpu.VMEM(x_shape, BF16),
            pltpu.VMEM((6, 8, 64, TILE), F32),
            pltpu.VMEM((6, 7, 64, TILE), BF16), pltpu.VMEM((6, 7, 64, TILE), BF16),
            pltpu.VMEM((2, 8, 3, 8, TILE), F32), pltpu.VMEM((2, 7, 3, 8, TILE), F32),
            pltpu.VMEM((2, 16, TILE), F32), pltpu.VMEM((2, 16, TILE), F32),
            dma, dma((4,)), dma, dma((4,)), dma, dma((28,)), dma, dma((28,)), dma, dma((12,)),
            dma((6,)), dma((6,)), dma((2,)), dma((2,)), dma((2,)),
        ],
        compiler_params=pltpu.CompilerParams(collective_id=0, has_side_effects=True, vmem_limit_bytes=56 * 2**20),
        cost_estimate=pl.CostEstimate(flops=2 * 384 * 256 * 8192, bytes_accessed=4 * 2**20, transcendentals=0),
    )(valid_rows, activations, gradients)
    out = jax.ShapeDtypeStruct((12, 2, TILE), F32)
    return pl.pallas_call(arrange, out_shape=(out, out), in_specs=[vmem], out_specs=(vmem, vmem))(both)


def solution(mesh):
    placed = (P(("dp", "ctx"), None), P(("dp", "ctx"), None), P())
    return jax.shard_map(
        body,
        mesh=mesh,
        in_specs=placed,
        out_specs=(P("dp", None, "ctx"), P("dp", None, "ctx")),
        check_vma=False,
    )
```

```python
import jax
import jax.numpy as jnp
from jax import lax
from jax.experimental import pallas as pl
from jax.experimental.pallas import tpu as pltpu
from jax.sharding import PartitionSpec as P

MESH = pl.DeviceIdType.MESH
F32, BF16 = jnp.float32, jnp.bfloat16
WIN, ROWS, TILE = 384, 128, 256
NX, NY, NZ = 4, 8, 8
AXES = {"x": (0, NX), "y": (1, NY), "z": (2, NZ)}
PARTS = ("y", "z", "x")
ROW0 = {"y": 0, "z": 128, "x": 256}
SECOND = {("y", 0): "x", ("y", 1): "x", ("z", 0): "x", ("z", 1): "x", ("x", 0): "y", ("x", 1): "z"}
STREAMS = tuple(SECOND)


def place():
    dp, ctx = lax.axis_index("dp"), lax.axis_index("ctx")
    x = lax.div(ctx, 8) * 2 + lax.rem(lax.div(dp, 2), 2)
    return x, lax.rem(ctx, 8), lax.div(dp, 4), lax.rem(dp, 2)


def device(x, y, z, core):
    return (z * 4 + lax.rem(x, 2) * 2 + core, lax.div(x, 2) * 8 + y)


def chain_length(n, q, way):
    return n // 2 if q % 2 == way else n // 2 - 1


def kernel(
    live, acts, grads, out,
    rows_ref, held, wins, prods, send_y, recv_y, send_z, recv_z, send_x, recv_x,
    sums, send_two, recv_two, three, recv_three,
    live_sem, own_sem, in_send, in_recv, y_send, y_recv, z_send, z_recv, x_send, x_recv,
    two_send, two_recv, three_send, three_recv,
):
    here = place()
    x, y, z, core = here
    partner = device(x, y, z, 1 - core)

    def moved(axis, by, to=core):
        at, n = AXES[axis]
        there = [x, y, z, to]
        there[at] = lax.rem(here[at] + (by % n), n)
        return there[at], device(*there)

    def own_copy(array, q):
        cols = pl.ds(q * 2048, 2048)
        return pltpu.make_async_copy(array.at[:, cols], held.at[0, :, cols], own_sem.at[q])

    def swap_copy(array, q):
        cols = pl.ds(q * 2048, 2048)
        return pltpu.make_async_remote_copy(
            src_ref=array.at[:, cols], dst_ref=held.at[1, :, cols], send_sem=in_send, recv_sem=in_recv.at[q],
            device_id=partner, device_id_type=MESH,
        )

    @pl.when(core == 0)
    def _():
        for q in range(4):
            own_copy(acts, q).start()

    @pl.when(core == 1)
    def _():
        for q in range(4):
            own_copy(grads, q).start()

    live_copy = pltpu.make_async_copy(live, rows_ref, live_sem)
    live_copy.start()
    barrier = pltpu.get_barrier_semaphore()
    peers = [partner] + [moved("x", by)[1] for by in range(1, NX)]
    peers += [moved(axis, by, to)[1] for axis in "yz" for by in range(1, 8) for to in range(2)]
    for peer in peers:
        pl.semaphore_signal(barrier, inc=1, device_id=peer, device_id_type=MESH)

    def swap():
        pl.semaphore_wait(barrier, len(peers))

        @pl.when(core == 0)
        def _():
            for q in range(4):
                swap_copy(grads, q).start()

        @pl.when(core == 1)
        def _():
            for q in range(4):
                swap_copy(acts, q).start()

    ctx = lax.axis_index("ctx")
    group = lax.axis_index("dp")

    def window(k, group):
        live = rows_ref[group] - ctx * ROWS
        keep = lax.broadcasted_iota(jnp.int32, (ROWS, WIN), 0) < live
        win = jnp.where(keep, held[k, :, :WIN].astype(F32), 0.0).T
        for i, part in enumerate(PARTS):
            order = [(zz, lo) for zz in range(8) for lo in range(2)]
            if part != "z":
                order = [(zz, lo) for lo in range(2) for zz in range(8)]
            at = [zz * 48 + lo * 24 + i * 8 for zz, lo in order]
            wins[k, ROW0[part] : ROW0[part] + 128, :] = jnp.concatenate([win[r : r + 8] for r in at]).astype(BF16)

    def products(k, q):
        def one(i, carry):
            t = q * 8 + i
            cols = held[k, :, pl.ds(pl.multiple_of(t * TILE, TILE), TILE)]
            prods[k, t] = jnp.dot(wins[k], cols, preferred_element_type=F32).astype(BF16)
            return carry

        lax.fori_loop(0, 8, one, 0, unroll=4)

    def own(part, q, dest):
        def half(k):
            if part == "y":
                return prods[k, q * 8 + dest, 0:128, :].astype(F32)
            if part == "z":
                return prods[k, q * 8 : q * 8 + 8, pl.ds(pl.multiple_of(128 + dest * 16, 16), 16), :].astype(F32)
            at = pl.multiple_of(256 + lax.rem(dest, 2) * 64, 64)
            tile = (q // 2) * 16 + lax.div(dest, 2) * 8 + (q % 2) * 4
            return prods[k, pl.ds(tile, 4), pl.ds(at, 64), :].astype(F32)

        return half(0) + half(1)

    chain = {"y": (send_y, recv_y, y_send, y_recv), "z": (send_z, recv_z, z_send, z_recv), "x": (send_x, recv_x, x_send, x_recv)}

    def drain(ref, sem):
        pltpu.make_async_copy(ref, ref, sem).wait()

    def slot(part, q, way, k):
        far = AXES[part][1] // 2
        return q * (2 * far - 1) + (0 if q % 2 == way else far) + k - 1

    def chain_copy(part, q, way, k):
        src, dst, ssem, rsem = chain[part]
        at = slot(part, q, way, k)
        return pltpu.make_async_remote_copy(
            src_ref=src.at[at], dst_ref=dst.at[at], send_sem=ssem, recv_sem=rsem.at[at],
            device_id=moved(part, 1 if way == 0 else -1)[1], device_id_type=MESH,
        )

    def hop(part, q, way, k):
        n = AXES[part][1]
        dest, _ = moved(part, k if way == 0 else -k)
        value = own(part, q, dest)
        if k < chain_length(n, q, way):
            chain_copy(part, q, way, k + 1).wait_recv()
            value = value + chain[part][1][slot(part, q, way, k + 1)].astype(F32)
        chain[part][0][slot(part, q, way, k)] = value.astype(BF16)
        chain_copy(part, q, way, k).start()

    def finish(part, q):
        for way in range(2):
            chain_copy(part, q, way, 1).wait_recv()
        value = own(part, q, here[AXES[part][0]])
        for way in range(2):
            value = value + chain[part][1][slot(part, q, way, 1)].astype(F32)
        h, low = q // 2, q % 2
        s = STREAMS.index((part, h))
        if part == "y":
            sums[s, low * 2 : low * 2 + 2] = value.reshape(2, 64, TILE)
        elif part == "z":
            for yy in range(8):
                sums[s, low * 2 : low * 2 + 2, yy * 8 : yy * 8 + 8, :] = value[yy].reshape(2, 8, TILE)
        elif h == 0:
            sums[s, low * 4 : low * 4 + 4] = value
        else:
            for i in range(4):
                at = (low * 4 + i) * 8
                sums[s, :, at : at + 8, :] = value[i].reshape(8, 8, TILE)

    def far_first(n):
        return sorted(range(1, n), key=lambda k: -min(k, n - k))

    def two_copy(s, k):
        return pltpu.make_async_remote_copy(
            src_ref=send_two.at[s, k - 1], dst_ref=recv_two.at[s, k - 1], send_sem=two_send.at[s],
            recv_sem=two_recv.at[s], device_id=moved(SECOND[STREAMS[s]], k)[1], device_id_type=MESH,
        )

    def spread(s):
        axis = SECOND[STREAMS[s]]
        for k in far_first(AXES[axis][1]):
            send_two[s, k - 1] = sums[s, moved(axis, k)[0]].astype(BF16)
            two_copy(s, k).start()

    def gather(s):
        at, n = AXES[SECOND[STREAMS[s]]]
        value = sums[s, here[at]]
        drain(recv_two.at[s, pl.ds(0, n - 1)], two_recv.at[s])
        for k in range(1, n):
            value = value + recv_two[s, k - 1].astype(F32)
        return value.reshape(8, 8, TILE)

    blocks = ((pl.ds(0, 2), pl.ds(2, 1)), (pl.ds(0, 1), pl.ds(1, 2)))

    def three_copy(g, k, to, source):
        dest, there = moved("zy"[g], k, to)
        which = blocks[g][to]
        return pltpu.make_async_remote_copy(
            src_ref=three.at[g, dest, which], dst_ref=recv_three.at[source, g, k, which], send_sem=three_send.at[to, g],
            recv_sem=three_recv.at[source, g], device_id=there, device_id_type=MESH,
        )

    swap()
    live_copy.wait()
    for q in range(4):
        own_copy(acts, q).wait()
        if q == 0:
            window(0, group)
            products(0, 0)
        if q == 1:
            products(0, 1)
    for q in range(4):
        if q > 1:
            products(0, q)
        swap_copy(acts, q).wait_recv()
        if q == 0:
            window(1, group + 1 - 2 * core)
        products(1, q)
        far = q % 2
        for part in "zy":
            hop(part, q, far, 4)
            hop(part, q, 1 - far, 3)
        if q % 2 == 1:
            for low in range(2):
                hop("x", q - 1 + low, low, 2)
                hop("x", q - 1 + low, 1 - low, 1)
    for k in (3, 2, 1):
        for q in range(4):
            for part in "zy":
                hop(part, q, q % 2, k)
            if k == 2:
                hop("x", q, q % 2, 1)
        if k > 1:
            for q in range(4):
                for part in "zy":
                    hop(part, q, 1 - q % 2, k - 1)

    for part in "yzx":
        for h in range(2):
            for q in (2 * h, 2 * h + 1):
                finish(part, q)
            spread(STREAMS.index((part, h)))
    drain(held.at[1], in_send)
    for part in PARTS:
        drain(chain[part][0], chain[part][2])
    def start_three(g):
        for k in far_first(8):
            for to in range(2):
                three_copy(g, k, to, core).start()
        for to in range(2):

            @pl.when(core != to)
            def _():
                three_copy(g, 0, to, core).start()

    for h in range(2):
        three[0, :, h] = gather(STREAMS.index(("y", h)))
    both = [gather(STREAMS.index(("z", h))) for h in range(2)]
    for i in range(2):
        three[1, :, i] = jnp.concatenate([part[:, i * 4 : i * 4 + 4] for part in both], axis=1)
    three[0, :, 2] = gather(STREAMS.index(("x", 0)))
    start_three(0)
    three[1, :, 2] = gather(STREAMS.index(("x", 1)))
    start_three(1)
    for s, stream in enumerate(STREAMS):
        drain(send_two.at[s, pl.ds(0, AXES[SECOND[stream]][1] - 1)], two_send.at[s])

    total = rows_ref[0]
    for i in range(1, 32):
        total = total + rows_ref[i]
    total = total.astype(F32)
    for c in range(2):

        @pl.when(core == c)
        def _():
            for array in (c, 1 - c):
                done = []
                for g in range(2):
                    which = blocks[g][c]
                    first = 1 if array == c else 0
                    drain(recv_three.at[array, g, pl.ds(first, 8 - first), which], three_recv.at[array, g])
                    if array == c:
                        value = three[g, here[AXES["zy"[g]][0]], which]
                    else:
                        value = recv_three[array, g, 0, which]
                    for k in range(1, 8):
                        value = value + recv_three[array, g, k, which]
                    done.append(value)
                for h in range(2):
                    if c == 0:
                        block = [done[0][h], done[1][0, h * 4 : h * 4 + 4]]
                    else:
                        block = [done[1][0, h * 4 : h * 4 + 4], done[0][0] if h == 0 else done[1][1]]
                    out[array, h] = jnp.concatenate(block) / total
            for g in range(2):
                for to in range(2):
                    first = 1 if to == c else 0
                    drain(recv_three.at[0, g, pl.ds(first, 8 - first), blocks[g][to]], three_send.at[to, g])


def arrange(both, out_a, out_g):
    for h in range(2):
        out_a[:, h, :] = both[0, h]
        out_g[:, h, :] = both[1, h]


def body(activations, gradients, valid_rows):
    dma = pltpu.SemaphoreType.DMA
    vmem = pl.BlockSpec(memory_space=pltpu.VMEM)
    y_shape, z_shape, x_shape = (28, 128, TILE), (28, 8, 16, TILE), (12, 4, 64, TILE)
    both = pl.pallas_call(
        kernel,
        out_shape=jax.ShapeDtypeStruct((2, 2, 12, TILE), F32),
        in_specs=[
            pl.BlockSpec(memory_space=pl.ANY),
            pl.BlockSpec(memory_space=pl.ANY),
            pl.BlockSpec(memory_space=pl.ANY),
        ],
        out_specs=vmem,
        scratch_shapes=[
            pltpu.SMEM((32,), jnp.int32),
            pltpu.VMEM((2, ROWS, 8192), BF16),
            pltpu.VMEM((2, WIN, ROWS), BF16),
            pltpu.VMEM((2, 32, WIN, TILE), BF16),
            pltpu.VMEM(y_shape, BF16), pltpu.VMEM(y_shape, BF16),
            pltpu.VMEM(z_shape, BF16), pltpu.VMEM(z_shape, BF16),
            pltpu.VMEM(x_shape, BF16), pltpu.VMEM(x_shape, BF16),
            pltpu.VMEM((6, 8, 64, TILE), F32),
            pltpu.VMEM((6, 7, 64, TILE), BF16), pltpu.VMEM((6, 7, 64, TILE), BF16),
            pltpu.VMEM((2, 8, 3, 8, TILE), F32), pltpu.VMEM((2, 2, 8, 3, 8, TILE), F32),
            dma, dma((4,)), dma, dma((4,)), dma, dma((28,)), dma, dma((28,)), dma, dma((12,)),
            dma((6,)), dma((6,)), dma((2, 2)), dma((2, 2)),
        ],
        compiler_params=pltpu.CompilerParams(collective_id=0, has_side_effects=True, vmem_limit_bytes=56 * 2**20),
        cost_estimate=pl.CostEstimate(flops=2 * 384 * 256 * 8192, bytes_accessed=4 * 2**20, transcendentals=0),
    )(valid_rows, activations, gradients)
    out = jax.ShapeDtypeStruct((12, 2, TILE), F32)
    return pl.pallas_call(arrange, out_shape=(out, out), in_specs=[vmem], out_specs=(vmem, vmem))(both)


def solution(mesh):
    placed = (P(("dp", "ctx"), None), P(("dp", "ctx"), None), P())
    return jax.shard_map(
        body,
        mesh=mesh,
        in_specs=placed,
        out_specs=(P("dp", None, "ctx"), P("dp", None, "ctx")),
        check_vma=False,
    )
```

```python
import jax
import jax.numpy as jnp
from jax import lax
from jax.experimental import pallas as pl
from jax.experimental.pallas import tpu as pltpu
from jax.sharding import PartitionSpec as P

MESH = pl.DeviceIdType.MESH
F32, BF16 = jnp.float32, jnp.bfloat16
WIN, ROWS, TILE = 384, 128, 256
NX, NY, NZ = 4, 8, 8
AXES = {"x": (0, NX), "y": (1, NY), "z": (2, NZ)}
PARTS = ("y", "z", "x")
ROW0 = {"y": 0, "z": 128, "x": 256}
SECOND = {("y", 0): "x", ("y", 1): "x", ("z", 0): "x", ("z", 1): "x", ("x", 0): "y", ("x", 1): "z"}
STREAMS = tuple(SECOND)


def place():
    dp, ctx = lax.axis_index("dp"), lax.axis_index("ctx")
    x = lax.div(ctx, 8) * 2 + lax.rem(lax.div(dp, 2), 2)
    return x, lax.rem(ctx, 8), lax.div(dp, 4), lax.rem(dp, 2)


def device(x, y, z, core):
    return (z * 4 + lax.rem(x, 2) * 2 + core, lax.div(x, 2) * 8 + y)


def chain_length(n, q, way):
    return n // 2 if q % 2 == way else n // 2 - 1


def kernel(
    live, acts, grads, out,
    rows_ref, held, wins, prods, send_y, recv_y, send_z, recv_z, send_x, recv_x,
    sums, send_two, recv_two, three, recv_three,
    live_sem, own_sem, in_send, in_recv, y_send, y_recv, z_send, z_recv, x_send, x_recv,
    two_send, two_recv, three_send, three_recv,
):
    here = place()
    x, y, z, core = here
    partner = device(x, y, z, 1 - core)

    def moved(axis, by, to=core):
        at, n = AXES[axis]
        there = [x, y, z, to]
        there[at] = lax.rem(here[at] + (by % n), n)
        return there[at], device(*there)

    def own_copy(array, q):
        cols = pl.ds(q * 2048, 2048)
        return pltpu.make_async_copy(array.at[:, cols], held.at[0, :, cols], own_sem.at[q])

    def swap_copy(array, q):
        cols = pl.ds(q * 2048, 2048)
        return pltpu.make_async_remote_copy(
            src_ref=array.at[:, cols], dst_ref=held.at[1, :, cols], send_sem=in_send, recv_sem=in_recv.at[q],
            device_id=partner, device_id_type=MESH,
        )

    @pl.when(core == 0)
    def _():
        for q in range(4):
            own_copy(acts, q).start()

    @pl.when(core == 1)
    def _():
        for q in range(4):
            own_copy(grads, q).start()

    live_copy = pltpu.make_async_copy(live, rows_ref, live_sem)
    live_copy.start()
    barrier = pltpu.get_barrier_semaphore()
    peers = [partner] + [moved("x", by)[1] for by in range(1, NX)]
    peers += [moved(axis, by, to)[1] for axis in "yz" for by in range(1, 8) for to in range(2)]
    for peer in peers:
        pl.semaphore_signal(barrier, inc=1, device_id=peer, device_id_type=MESH)

    def swap():
        pl.semaphore_wait(barrier, len(peers))

        @pl.when(core == 0)
        def _():
            for q in range(4):
                swap_copy(grads, q).start()

        @pl.when(core == 1)
        def _():
            for q in range(4):
                swap_copy(acts, q).start()

    ctx = lax.axis_index("ctx")
    group = lax.axis_index("dp")

    def window(k, group):
        live = rows_ref[group] - ctx * ROWS
        keep = lax.broadcasted_iota(jnp.int32, (ROWS, WIN), 0) < live
        win = jnp.where(keep, held[k, :, :WIN].astype(F32), 0.0).T
        for i, part in enumerate(PARTS):
            order = [(zz, lo) for zz in range(8) for lo in range(2)]
            if part != "z":
                order = [(zz, lo) for lo in range(2) for zz in range(8)]
            at = [zz * 48 + lo * 24 + i * 8 for zz, lo in order]
            wins[k, ROW0[part] : ROW0[part] + 128, :] = jnp.concatenate([win[r : r + 8] for r in at]).astype(BF16)

    def products(k, q):
        def one(i, carry):
            t = q * 8 + i
            cols = held[k, :, pl.ds(pl.multiple_of(t * TILE, TILE), TILE)]
            prods[k, t] = jnp.dot(wins[k], cols, preferred_element_type=F32).astype(BF16)
            return carry

        lax.fori_loop(0, 8, one, 0, unroll=4)

    def own(part, q, dest):
        def half(k):
            if part == "y":
                return prods[k, q * 8 + dest, 0:128, :].astype(F32)
            if part == "z":
                return prods[k, q * 8 : q * 8 + 8, pl.ds(pl.multiple_of(128 + dest * 16, 16), 16), :].astype(F32)
            at = pl.multiple_of(256 + lax.rem(dest, 2) * 64, 64)
            tile = (q // 2) * 16 + lax.div(dest, 2) * 8 + (q % 2) * 4
            return prods[k, pl.ds(tile, 4), pl.ds(at, 64), :].astype(F32)

        return half(0) + half(1)

    chain = {"y": (send_y, recv_y, y_send, y_recv), "z": (send_z, recv_z, z_send, z_recv), "x": (send_x, recv_x, x_send, x_recv)}

    def drain(ref, sem):
        pltpu.make_async_copy(ref, ref, sem).wait()

    def slot(part, q, way, k):
        far = AXES[part][1] // 2
        return q * (2 * far - 1) + (0 if q % 2 == way else far) + k - 1

    def chain_copy(part, q, way, k):
        src, dst, ssem, rsem = chain[part]
        at = slot(part, q, way, k)
        return pltpu.make_async_remote_copy(
            src_ref=src.at[at], dst_ref=dst.at[at], send_sem=ssem, recv_sem=rsem.at[at],
            device_id=moved(part, 1 if way == 0 else -1)[1], device_id_type=MESH,
        )

    def hop(part, q, way, k):
        n = AXES[part][1]
        dest, _ = moved(part, k if way == 0 else -k)
        value = own(part, q, dest)
        if k < chain_length(n, q, way):
            chain_copy(part, q, way, k + 1).wait_recv()
            value = value + chain[part][1][slot(part, q, way, k + 1)].astype(F32)
        chain[part][0][slot(part, q, way, k)] = value.astype(BF16)
        chain_copy(part, q, way, k).start()

    def finish(part, q):
        for way in range(2):
            chain_copy(part, q, way, 1).wait_recv()
        value = own(part, q, here[AXES[part][0]])
        for way in range(2):
            value = value + chain[part][1][slot(part, q, way, 1)].astype(F32)
        h, low = q // 2, q % 2
        s = STREAMS.index((part, h))
        if part == "y":
            sums[s, low * 2 : low * 2 + 2] = value.reshape(2, 64, TILE)
        elif part == "z":
            for yy in range(8):
                sums[s, low * 2 : low * 2 + 2, yy * 8 : yy * 8 + 8, :] = value[yy].reshape(2, 8, TILE)
        elif h == 0:
            sums[s, low * 4 : low * 4 + 4] = value
        else:
            for i in range(4):
                at = (low * 4 + i) * 8
                sums[s, :, at : at + 8, :] = value[i].reshape(8, 8, TILE)

    def far_first(n):
        return sorted(range(1, n), key=lambda k: -min(k, n - k))

    def two_copy(s, k):
        return pltpu.make_async_remote_copy(
            src_ref=send_two.at[s, k - 1], dst_ref=recv_two.at[s, k - 1], send_sem=two_send.at[s],
            recv_sem=two_recv.at[s], device_id=moved(SECOND[STREAMS[s]], k)[1], device_id_type=MESH,
        )

    def spread(s):
        axis = SECOND[STREAMS[s]]
        for k in far_first(AXES[axis][1]):
            send_two[s, k - 1] = sums[s, moved(axis, k)[0]].astype(BF16)
            two_copy(s, k).start()

    def gather(s):
        at, n = AXES[SECOND[STREAMS[s]]]
        value = sums[s, here[at]]
        drain(recv_two.at[s, pl.ds(0, n - 1)], two_recv.at[s])
        for k in range(1, n):
            value = value + recv_two[s, k - 1].astype(F32)
        return value.reshape(8, 8, TILE)

    blocks = ((pl.ds(0, 2), pl.ds(2, 1)), (pl.ds(0, 1), pl.ds(1, 2)))

    def three_copy(g, k, to, source):
        dest, there = moved("zy"[g], k, to)
        which = blocks[g][to]
        return pltpu.make_async_remote_copy(
            src_ref=three.at[g, dest, which], dst_ref=recv_three.at[source, g, k, which], send_sem=three_send.at[to, g],
            recv_sem=three_recv.at[source, g], device_id=there, device_id_type=MESH,
        )

    swap()
    live_copy.wait()
    for q in range(4):
        own_copy(acts, q).wait()
        if q == 0:
            window(0, group)
            products(0, 0)
        if q == 1:
            products(0, 1)
    for q in range(4):
        if q > 1:
            products(0, q)
        swap_copy(acts, q).wait_recv()
        if q == 0:
            window(1, group + 1 - 2 * core)
        products(1, q)
        far = q % 2
        for part in "zy":
            hop(part, q, far, 4)
            hop(part, q, 1 - far, 3)
        if q % 2 == 1:
            for low in range(2):
                hop("x", q - 1 + low, low, 2)
                hop("x", q - 1 + low, 1 - low, 1)
    for k in (3, 2, 1):
        for q in range(4):
            for part in "zy":
                hop(part, q, q % 2, k)
            if k == 2:
                hop("x", q, q % 2, 1)
        if k > 1:
            for q in range(4):
                for part in "zy":
                    hop(part, q, 1 - q % 2, k - 1)

    for part in "yzx":
        for h in range(2):
            for q in (2 * h, 2 * h + 1):
                finish(part, q)
            spread(STREAMS.index((part, h)))
    drain(held.at[1], in_send)
    for part in PARTS:
        drain(chain[part][0], chain[part][2])
    def start_three(g, to):
        for k in far_first(8):
            three_copy(g, k, to, core).start()

        @pl.when(core != to)
        def _():
            three_copy(g, 0, to, core).start()

    for h in range(2):
        three[0, :, h] = gather(STREAMS.index(("y", h)))
    start_three(0, 0)
    both = [gather(STREAMS.index(("z", h))) for h in range(2)]
    for i in range(2):
        three[1, :, i] = jnp.concatenate([part[:, i * 4 : i * 4 + 4] for part in both], axis=1)
    start_three(1, 0)
    three[0, :, 2] = gather(STREAMS.index(("x", 0)))
    start_three(0, 1)
    three[1, :, 2] = gather(STREAMS.index(("x", 1)))
    start_three(1, 1)
    for s, stream in enumerate(STREAMS):
        drain(send_two.at[s, pl.ds(0, AXES[SECOND[stream]][1] - 1)], two_send.at[s])

    total = rows_ref[0]
    for i in range(1, 32):
        total = total + rows_ref[i]
    total = total.astype(F32)
    for c in range(2):

        @pl.when(core == c)
        def _():
            for array in (c, 1 - c):
                done = []
                for g in range(2):
                    which = blocks[g][c]
                    first = 1 if array == c else 0
                    drain(recv_three.at[array, g, pl.ds(first, 8 - first), which], three_recv.at[array, g])
                    if array == c:
                        value = three[g, here[AXES["zy"[g]][0]], which]
                    else:
                        value = recv_three[array, g, 0, which]
                    for k in range(1, 8):
                        value = value + recv_three[array, g, k, which]
                    done.append(value)
                for h in range(2):
                    if c == 0:
                        block = [done[0][h], done[1][0, h * 4 : h * 4 + 4]]
                    else:
                        block = [done[1][0, h * 4 : h * 4 + 4], done[0][0] if h == 0 else done[1][1]]
                    out[array, h] = jnp.concatenate(block) / total
            for g in range(2):
                for to in range(2):
                    first = 1 if to == c else 0
                    drain(recv_three.at[0, g, pl.ds(first, 8 - first), blocks[g][to]], three_send.at[to, g])


def arrange(both, out_a, out_g):
    for h in range(2):
        out_a[:, h, :] = both[0, h]
        out_g[:, h, :] = both[1, h]


def body(activations, gradients, valid_rows):
    dma = pltpu.SemaphoreType.DMA
    vmem = pl.BlockSpec(memory_space=pltpu.VMEM)
    y_shape, z_shape, x_shape = (28, 128, TILE), (28, 8, 16, TILE), (12, 4, 64, TILE)
    both = pl.pallas_call(
        kernel,
        out_shape=jax.ShapeDtypeStruct((2, 2, 12, TILE), F32),
        in_specs=[
            pl.BlockSpec(memory_space=pl.ANY),
            pl.BlockSpec(memory_space=pl.ANY),
            pl.BlockSpec(memory_space=pl.ANY),
        ],
        out_specs=vmem,
        scratch_shapes=[
            pltpu.SMEM((32,), jnp.int32),
            pltpu.VMEM((2, ROWS, 8192), BF16),
            pltpu.VMEM((2, WIN, ROWS), BF16),
            pltpu.VMEM((2, 32, WIN, TILE), BF16),
            pltpu.VMEM(y_shape, BF16), pltpu.VMEM(y_shape, BF16),
            pltpu.VMEM(z_shape, BF16), pltpu.VMEM(z_shape, BF16),
            pltpu.VMEM(x_shape, BF16), pltpu.VMEM(x_shape, BF16),
            pltpu.VMEM((6, 8, 64, TILE), F32),
            pltpu.VMEM((6, 7, 64, TILE), BF16), pltpu.VMEM((6, 7, 64, TILE), BF16),
            pltpu.VMEM((2, 8, 3, 8, TILE), F32), pltpu.VMEM((2, 2, 8, 3, 8, TILE), F32),
            dma, dma((4,)), dma, dma((4,)), dma, dma((28,)), dma, dma((28,)), dma, dma((12,)),
            dma((6,)), dma((6,)), dma((2, 2)), dma((2, 2)),
        ],
        compiler_params=pltpu.CompilerParams(collective_id=0, has_side_effects=True, vmem_limit_bytes=56 * 2**20),
        cost_estimate=pl.CostEstimate(flops=2 * 384 * 256 * 8192, bytes_accessed=4 * 2**20, transcendentals=0),
    )(valid_rows, activations, gradients)
    out = jax.ShapeDtypeStruct((12, 2, TILE), F32)
    return pl.pallas_call(arrange, out_shape=(out, out), in_specs=[vmem], out_specs=(vmem, vmem))(both)


def solution(mesh):
    placed = (P(("dp", "ctx"), None), P(("dp", "ctx"), None), P())
    return jax.shard_map(
        body,
        mesh=mesh,
        in_specs=placed,
        out_specs=(P("dp", None, "ctx"), P("dp", None, "ctx")),
        check_vma=False,
    )
```
